1024 devices in a mesh: gy: 8 (over y), gx: 128 (over x, z, core).
Axes of the slice: x: 8, y: 8, z: 8, core: 2. Of those that a mesh axis runs over, the one named last changes fastest.
Arguments:
- cotangent: float32 [3, 64, 2048, 256], P(None, 'gy', 'gx'), may hold values from -8 to 8
- coefficient: float32 [64, 2048, 256], P('gy', 'gx'), may hold values from 0.05 to 4
Outputs:
- velocity_grad: float32 [3, 64, 2048, 256], P(None, 'gy', 'gx')
- adjoint_pressure: float32 [64, 2048, 256], P('gy', 'gx')
The draws below stay inside these ranges and needn't reach their ends.
All inputs are finite; a program needn't handle non-finite values.
Results may differ from the reference program's by a relative error of at most 0.0025.
Values sent between devices are 32-bit elements; how exact they have to be, the bound alone decides.
No kernel may reach another device: no remote copies, remote signals or barrier semaphores. Data moves between devices by JAX's collectives and lax.ppermute only.
A program may use at most 32 MiB of HBM per device.

```python
import math
import jax
import jax.numpy as jnp

NZ = 256
ITERS = 4
NY = 64
NX = 2048


def position_trend(ny_cells, nx_cells, x_weight):
    along_y = jnp.arange(ny_cells, dtype=jnp.float32) / max(ny_cells - 1, 1)
    along_x = jnp.arange(nx_cells, dtype=jnp.float32) / max(nx_cells - 1, 1)
    return x_weight * along_x[None, :, None] + (1.0 - x_weight) * along_y[:, None, None]


def rising_scale(ny_cells, nx_cells, base, rise_y, rise_x):
    along_y = jnp.arange(ny_cells, dtype=jnp.float32) / max(ny_cells - 1, 1)
    along_x = jnp.arange(nx_cells, dtype=jnp.float32) / max(nx_cells - 1, 1)
    return base * jnp.exp(math.log(rise_y) * along_y[:, None, None] + math.log(rise_x) * along_x[None, :, None])


def draw_cotangent(key, part):
    key = jax.random.fold_in(key, 11)
    values = jax.random.truncated_normal(key, -4.0, 4.0, (3, NY, NX, NZ), jnp.float32)
    scale = rising_scale(NY, NX, 0.22, 3.0, 3.0)
    return (values * scale[None]).astype(jnp.float32)


def draw_coefficient(key, part):
    key = jax.random.fold_in(key, 23)
    trend = position_trend(NY, NX, 0.5)
    rough = jax.random.uniform(key, (NY, NX, NZ), jnp.float32, 0.0, 1.0)
    mixed = 0.6 * trend + 0.4 * rough
    return (0.05 * jnp.exp(math.log(80.0) * mixed)).astype(jnp.float32)


def setup_inputs(seed: int = 0) -> dict:
    key_list = jax.random.split(jax.random.key(seed), 3)
    return {
        "cotangent": draw_cotangent(jax.random.fold_in(key_list[2], 71), 0),
        "coefficient": draw_coefficient(jax.random.fold_in(key_list[2], 71), 0),
    }


def lower_of(field, axis):
    widths = [(0, 0)] * field.ndim
    widths[axis] = (1, 0)
    padded = jnp.pad(field, widths)
    return lax_slice(padded, axis, 0, field.shape[axis])


def upper_of(field, axis):
    widths = [(0, 0)] * field.ndim
    widths[axis] = (0, 1)
    padded = jnp.pad(field, widths)
    return lax_slice(padded, axis, 1, field.shape[axis])


def lax_slice(array, axis, start, length):
    index = [slice(None)] * array.ndim
    index[axis] = slice(start, start + length)
    return array[tuple(index)]


def operate_on(field, scaling):
    beside = lower_of(field, 0) + upper_of(field, 0)
    beside = beside + lower_of(field, 1) + upper_of(field, 1)
    beside = beside + lower_of(field, 2) + upper_of(field, 2)
    return scaling * field - beside


def reference(cotangent, coefficient):
    source = (lower_of(cotangent[0], 0) - cotangent[0]) + (lower_of(cotangent[1], 1) - cotangent[1]) + (lower_of(cotangent[2], 2) - cotangent[2])
    scaling = 6.0 + coefficient
    residual = source
    precond = residual / scaling
    direction = precond
    energy = jnp.sum(residual * precond)
    adjoint = jnp.zeros_like(source)
    for sweep in range(ITERS):
        image = operate_on(direction, scaling)
        step_size = energy / jnp.sum(direction * image)
        adjoint = adjoint + step_size * direction
        if sweep + 1 < ITERS:
            residual = residual - step_size * image
            precond = residual / scaling
            fresh = jnp.sum(residual * precond)
            direction = precond + (fresh / energy) * direction
            energy = fresh
    velocity = jnp.stack([cotangent[0] + upper_of(adjoint, 0) - adjoint, cotangent[1] + upper_of(adjoint, 1) - adjoint, cotangent[2] + upper_of(adjoint, 2) - adjoint])
    return velocity, adjoint
```

```python
import functools

import jax
import jax.numpy as jnp
import numpy as np
from jax import lax
from jax.experimental import pallas as pl
from jax.experimental.pallas import tpu as pltpu
from jax.sharding import Mesh, PartitionSpec as P

ITERS = 4
HALO = ITERS
SHIFTS = (0.25, 1.0)
SPLIT = 0.6
NMOM = 2 * ITERS
AXES = ("y", "xh", "xl", "z", "c")
STAGE = (("xh", "z", "c"), ("y", "xl"))
F32 = jnp.float32


def iota(shape, axis):
    return lax.broadcasted_iota(jnp.int32, shape, axis)


def pack_kernel(cot, coef, t_out, d_out, up, down, right, left, up_r, up_l, down_r, down_l):
    ny, nx, nz = coef.shape
    sub, lane = iota((nx, nz), 0), iota((nx, nz), 1)
    sub8 = iota((8, nz), 0)
    column = jnp.zeros((8, nz), F32)
    for y in range(ny):
        c0, c1, c2 = cot[0, y], cot[1, y], cot[2, y]
        d = 1.0 / (6.0 + coef[y])
        t = jnp.where(sub == 0, 0.0, pltpu.roll(c1, 1, 0)) - c1
        t = t + (jnp.where(lane == 0, 0.0, pltpu.roll(c2, 1, 1)) - c2)
        t = t + ((cot[0, y - 1] - c0) if y else -c0)
        t_out[y] = t
        d_out[y] = d
        to_right = jnp.where(sub8 >= 4, t[nx - 8 :], pltpu.roll(d[nx - 8 :], 4, 0))
        to_left = jnp.where(sub8 < 4, t[:8], pltpu.roll(d[:8], 4, 0))
        right[y] = to_right
        left[y] = to_left
        if y < HALO:
            down[y], down[HALO + y] = t, d
            down_r[y], down_l[y] = to_right, to_left
        if y >= ny - HALO:
            j = y - (ny - HALO)
            up[j], up[HALO + j] = t, d
            up_r[j], up_l[j] = to_right, to_left
        column = jnp.where(sub8 == y, jnp.broadcast_to(c1[nx - 1 : nx], (8, nz)), column)
    edge = cot[0, ny - 1]
    up[2 * HALO] = edge
    right[ny] = edge[nx - 8 :]
    left[ny] = edge[:8]
    up_r[HALO] = edge[nx - 8 :]
    up_l[HALO] = edge[:8]
    right[ny + 1] = column
    up_r[HALO + 1] = column
    down_r[HALO] = column
    wide = jnp.concatenate([column, jnp.zeros((nx - 8, nz), F32)], axis=0)
    up[2 * HALO + 1] = wide
    down[2 * HALO] = wide


def krylov_kernel(t_own, d_own, coef, up, right, r_s, r_n, r_l, r_r, r_sw, r_se, r_nw, r_ne, v, part, dw):
    ny, nx, nz = coef.shape
    sub8 = iota((8, nz), 0)
    lane = iota((nx + 8, nz), 1)
    low = sub8 < 4

    def at_first(col_ref_value, k):
        return jnp.where(sub8 == 0, jnp.broadcast_to(col_ref_value[k : k + 1], (8, nz)), 0.0)

    def assemble(row, t, d, from_left, from_right, edge, edge_side, col_low, col_high, k):
        t_side = jnp.where(low, from_right, from_left)
        d_side = pltpu.roll(jnp.where(low, from_left, from_right), 4, 0)
        if edge is not None:
            t = t + edge
            t_side = t_side + edge_side
        t_first = t[:8] + at_first(col_low, k)
        t_side = t_side + at_first(col_high, k)
        v[0, row, 0:8] = t_first * d[:8]
        v[0, row, 8:nx] = t[8:] * d[8:]
        v[0, row, nx : nx + 8] = t_side * d_side
        dw[row, 0:nx] = d
        dw[row, nx : nx + 8] = d_side

    own_low, own_high = r_l[ny + 1], right[ny + 1]
    for y in range(ny):
        edge = edge_side = None
        if y == 0:
            edge = r_s[2 * HALO]
            edge_side = jnp.where(low, r_se[HALO], r_sw[HALO])
        assemble(y, t_own[y], d_own[y], r_l[y], r_r[y], edge, edge_side, own_low, own_high, y)
    col_low, col_high = r_nw[HALO], r_n[2 * HALO][:8]
    for j in range(HALO):
        edge = edge_side = None
        if j == 0:
            edge = up[2 * HALO]
            edge_side = jnp.where(low, r_r[ny], r_l[ny])
        assemble(ny + j, r_n[j], r_n[HALO + j], r_nw[j], r_ne[j], edge, edge_side, col_low, col_high, j)
    col_low, col_high = r_sw[HALO + 1], r_s[2 * HALO + 1][:8]
    for j in range(HALO):
        assemble(
            ny + HALO + j, r_s[j], r_s[HALO + j], r_sw[j], r_se[j], None, None, col_low, col_high, ny - HALO + j
        )

    rows = ny + 2 * HALO

    def powered(k, row):
        row = row % rows
        x = v[k, row]
        beside = v[k, (row + 1) % rows] + v[k, (row - 1) % rows]
        beside = beside + (pltpu.roll(x, 1, 0) + pltpu.roll(x, nx + 7, 0))
        beside = beside + jnp.where(lane == 0, 0.0, pltpu.roll(x, 1, 1))
        beside = beside + jnp.where(lane == nz - 1, 0.0, pltpu.roll(x, nz - 1, 1))
        return x - dw[row] * beside

    for k in range(ITERS - 1):
        reach = HALO - 1 - k
        for row in range(-reach, ny + reach):
            v[k + 1, row % rows] = powered(k, row)
    total = [jnp.zeros((8, 128), F32) for _ in range(NMOM * len(SHIFTS))]
    for y in range(ny):
        scaling = 6.0 + coef[y]
        last = powered(ITERS - 1, y)
        for a in range(0, nx, 8):
            for b in range(0, nz, 128):
                m = scaling[a : a + 8, b : b + 128]
                base = [v[k, y, a : a + 8, b : b + 128] for k in range(ITERS)] + [last[a : a + 8, b : b + 128]]
                for i, mu in enumerate(SHIFTS):
                    level, shifted = base, [base[0]]
                    for _ in range(ITERS):
                        level = [hi - (lo if mu == 1.0 else mu * lo) for lo, hi in zip(level, level[1:])]
                        shifted.append(level[0])
                    for k in range(ITERS):
                        weighted = m * shifted[k]
                        n = i * NMOM + 2 * k
                        total[n] = total[n] + weighted * shifted[k]
                        total[n + 1] = total[n + 1] + weighted * shifted[k + 1]
    stacked = jnp.concatenate([jnp.sum(x, axis=0, keepdims=True) for x in total], axis=0)
    sums = jnp.sum(stacked, axis=1, keepdims=True)
    n = len(total)
    diagonal = iota((n, 128), 0) == iota((n, 128), 1)
    line = jnp.sum(jnp.where(diagonal, sums, 0.0), axis=0, keepdims=True)
    part[...] = jnp.broadcast_to(line[None], part.shape)


def coefficients(moments):
    nearer = moments[1] + (SHIFTS[0] - SPLIT) * moments[0] < 0.0
    mom = [jnp.where(nearer, a, b) for a, b in zip(moments[:NMOM], moments[NMOM:])]
    mu = jnp.where(nearer, SHIFTS[0], SHIFTS[1]).astype(F32)
    zero = jnp.zeros_like(mom[0])
    one = zero + 1.0

    def times(poly):
        return [(lo + mu * hi) for lo, hi in zip([zero] + poly, poly + [zero])]

    sigma, tau = mom, mom
    rho, pi, x = [one], [one], [zero] * ITERS
    energy, lead = mom[0], one
    for k in range(ITERS):
        image = [hi + mu * lo for lo, hi in zip(tau, tau[1:])]
        step = energy / (lead * image[k])
        step = jnp.where((step > 0.4) & (step < 200.0), step, 0.0)
        x = [a + step * b for a, b in zip(x, pi + [zero] * (ITERS - len(pi)))]
        if k + 1 < ITERS:
            sigma = [a - step * b for a, b in zip(sigma, image)]
            rho = [a - step * b for a, b in zip(rho + [zero], times(pi))]
            lead = lead * -step
            fresh = lead * sigma[k + 1]
            fresh = jnp.maximum(fresh, 0.0)
            grow = jnp.where(energy > 0.0, fresh / energy, 0.0)
            tau = [a + grow * b for a, b in zip(sigma, tau)]
            pi = [a + grow * b for a, b in zip(rho, pi + [zero])]
            energy = fresh
    for i in range(ITERS - 1):
        for j in range(ITERS - 2, i - 1, -1):
            x[j] = x[j] - mu * x[j + 1]
    return x


def finish_kernel(parts, v, cot, vel, adj):
    _, ny, nx, nz = cot.shape
    line = jnp.sum(parts[...], axis=0)
    spread = jnp.broadcast_to(line, (8, 128))
    lane = iota((8, 128), 1)
    moments = [
        jnp.sum(jnp.where(lane == n, spread, 0.0), axis=1, keepdims=True) for n in range(NMOM * len(SHIFTS))
    ]
    coef = [c[:1] for c in coefficients(moments)]
    lane = iota((nx, nz), 1)

    def pressure(row):
        total = coef[0] * v[0, row]
        for k in range(1, ITERS):
            total = total + coef[k] * v[k, row]
        return total

    here = pressure(0)
    for y in range(ny):
        above = pressure(y + 1)
        x = here[:nx]
        adj[y] = x
        vel[0, y] = cot[0, y] + above[:nx] - x
        vel[1, y] = cot[1, y] + pltpu.roll(here, nx + 7, 0)[:nx] - x
        vel[2, y] = cot[2, y] + jnp.where(lane == nz - 1, 0.0, pltpu.roll(x, nz - 1, 1)) - x
        here = above


def neighbour(x, dy, dx, ny, nx):
    pairs = [
        (a * nx + b, (a + dy) * nx + b + dx)
        for a in range(ny)
        for b in range(nx)
        if 0 <= a + dy < ny and 0 <= b + dx < nx
    ]
    return lax.ppermute(x, AXES, pairs)


def exchange_sum(x, axes):
    return jnp.sum(lax.all_to_all(x, axes, 0, 0), axis=0, keepdims=True)


def on_device(gy, gx, sizes, cotangent, coefficient):
    ny, nx, nz = coefficient.shape
    block = (ny, nx, nz)
    shapes = [
        block,
        block,
        (2 * HALO + 2, nx, nz),
        (2 * HALO + 1, nx, nz),
        (ny + 2, 8, nz),
        (ny + 1, 8, nz),
        (HALO + 2, 8, nz),
        (HALO + 1, 8, nz),
        (HALO + 1, 8, nz),
        (HALO, 8, nz),
    ]
    limit = pltpu.CompilerParams(vmem_limit_bytes=24 * 1024 * 1024)
    t, d, up, down, right, left, up_r, up_l, down_r, down_l = pl.pallas_call(
        pack_kernel,
        out_shape=[jax.ShapeDtypeStruct(s, F32) for s in shapes],
        compiler_params=limit,
        name="pack",
    )(cotangent, coefficient)
    send = functools.partial(neighbour, ny=gy, nx=gx)
    r_sw = send(up_r, 1, 1)
    r_se = send(up_l, 1, -1)
    r_nw = send(down_r, -1, 1)
    r_ne = send(down_l, -1, -1)
    r_s = send(up, 1, 0)
    r_n = send(down, -1, 0)
    r_l = send(right, 0, 1)
    r_r = send(left, 0, -1)
    first, second = (int(np.prod([sizes[a] for a in axes])) for axes in STAGE)
    rows, wide = ny + 2 * HALO, nx + 8
    v, part = pl.pallas_call(
        krylov_kernel,
        out_shape=[
            jax.ShapeDtypeStruct((ITERS, rows, wide, nz), F32),
            jax.ShapeDtypeStruct((first, 1, 128), F32),
        ],
        scratch_shapes=[pltpu.VMEM((rows, wide, nz), F32)],
        compiler_params=limit,
        name="krylov",
    )(t, d, coefficient, up, right, r_s, r_n, r_l, r_r, r_sw, r_se, r_nw, r_ne)
    part = exchange_sum(part, STAGE[0])
    part = lax.all_to_all(jnp.broadcast_to(part, (second, 1, 128)), STAGE[1], 0, 0)
    return tuple(
        pl.pallas_call(
            finish_kernel,
            out_shape=[
                jax.ShapeDtypeStruct(cotangent.shape, F32),
                jax.ShapeDtypeStruct(coefficient.shape, F32),
            ],
            compiler_params=limit,
            name="finish",
        )(part, v, cotangent)
    )


def solution(mesh):
    gy, gx = mesh.shape["gy"], mesh.shape["gx"]
    fine = Mesh(np.asarray(mesh.devices).reshape(gy, 2, gx // 32, 8, 2), AXES)
    along_x = AXES[1:]
    wide, flat = P(None, AXES[0], along_x, None), P(AXES[0], along_x, None)
    return jax.shard_map(
        functools.partial(on_device, gy, gx, dict(fine.shape)),
        mesh=fine,
        in_specs=(wide, flat),
        out_specs=(wide, flat),
        check_vma=False,
    )
```

```python
import functools

import jax
import jax.numpy as jnp
import numpy as np
from jax import lax
from jax.experimental import pallas as pl
from jax.experimental.pallas import tpu as pltpu
from jax.sharding import Mesh, PartitionSpec as P

ITERS = 4
HALO = ITERS
SHIFTS = (0.25, 1.0)
SPLIT = 0.6
NMOM = 2 * ITERS
AXES = ("y", "xh", "xl", "z", "c")
STAGE = (("xh", "z"), ("y", "xl", "c"))
F32 = jnp.float32


def iota(shape, axis):
    return lax.broadcasted_iota(jnp.int32, shape, axis)


def pack_kernel(cot_hbm, coef_hbm, t_out, d_out, scaling, up, down, cot, coef, sems):
    copies = [
        pltpu.make_async_copy(coef_hbm, coef, sems.at[0]),
        pltpu.make_async_copy(cot_hbm, cot, sems.at[1]),
    ]
    for copy in copies:
        copy.start()
    for copy in copies:
        copy.wait()
    ny, nx, nz = coef.shape
    sub, lane = iota((nx, nz), 0), iota((nx, nz), 1)
    column = jnp.zeros((nx, nz), F32)
    for y in range(ny):
        c0, c1, c2 = cot[0, y], cot[1, y], cot[2, y]
        m = 6.0 + coef[y]
        d = 1.0 / m
        t = jnp.where(sub == 0, 0.0, pltpu.roll(c1, 1, 0)) - c1
        t = t + (jnp.where(lane == 0, 0.0, pltpu.roll(c2, 1, 1)) - c2)
        t = t + ((cot[0, y - 1] - c0) if y else -c0)
        t_out[y] = t
        d_out[y] = d
        scaling[y] = m
        if y < HALO:
            down[y], down[HALO + y] = t, d
        if y >= ny - HALO:
            j = y - (ny - HALO)
            up[j], up[HALO + j] = t, d
        column = jnp.where(sub == y, jnp.broadcast_to(c1[nx - 1 : nx], (nx, nz)), column)
    up[2 * HALO] = cot[0, ny - 1]
    up[2 * HALO + 1] = column
    down[2 * HALO] = column


def window_rows(t_own, d_own, up, r_s, r_n):
    ny = t_own.shape[0]
    out = []
    for y in range(ny):
        t = t_own[y]
        out.append((t + r_s[2 * HALO] if y == 0 else t, d_own[y]))
    for j in range(HALO):
        t = r_n[j]
        out.append((t + up[2 * HALO] if j == 0 else t, r_n[HALO + j]))
    return out + [(r_s[j], r_s[HALO + j]) for j in range(HALO)]


def side_kernel(t_own, d_own, up, r_s, r_n, right, left):
    ny, nx, nz = t_own.shape
    low = iota((8, nz), 0) < 4
    for row, (t, d) in enumerate(window_rows(t_own, d_own, up, r_s, r_n)):
        right[row] = jnp.where(low, pltpu.roll(d[nx - 8 :], 4, 0), t[nx - 8 :])
        left[row] = jnp.where(low, t[:8], pltpu.roll(d[:8], 4, 0))
    rows = ny + 2 * HALO
    right[rows] = up[2 * HALO + 1, :8]
    right[rows + 1] = jnp.where(low, r_n[2 * HALO, :8], r_s[2 * HALO + 1, :8])


def krylov_kernel(t_own, d_own, scaling_own, up, right, r_s, r_n, r_l, r_r, v, part, dw):
    ny, nx, nz = t_own.shape
    sub8 = iota((8, nz), 0)
    lane = iota((nx + 8, nz), 1)
    low = sub8 < 4
    columns = [(r_l[ny + 2 * HALO + i], right[ny + 2 * HALO + i]) for i in range(2)]

    def at_first(column, k):
        return jnp.where(sub8 == 0, jnp.broadcast_to(column[k : k + 1], (8, nz)), 0.0)

    for row, (t, d) in enumerate(window_rows(t_own, d_own, up, r_s, r_n)):
        before, after = columns[row // 8]
        v[0, row, 0:8] = (t[:8] + at_first(before, row % 8)) * d[:8]
        v[0, row, 8:nx] = t[8:] * d[8:]
        t = jnp.where(low, r_r[row], r_l[row]) + at_first(after, row % 8)
        d_side = pltpu.roll(jnp.where(low, r_l[row], r_r[row]), 4, 0)
        v[0, row, nx : nx + 8] = t * d_side
        dw[row, 0:nx] = d
        dw[row, nx : nx + 8] = d_side

    rows = ny + 2 * HALO

    def powered(k, row):
        row = row % rows
        x = v[k, row]
        beside = v[k, (row + 1) % rows] + v[k, (row - 1) % rows]
        beside = beside + (pltpu.roll(x, 1, 0) + pltpu.roll(x, nx + 7, 0))
        beside = beside + jnp.where(lane == 0, 0.0, pltpu.roll(x, 1, 1))
        beside = beside + jnp.where(lane == nz - 1, 0.0, pltpu.roll(x, nz - 1, 1))
        return x - dw[row] * beside

    for k in range(ITERS - 1):
        reach = HALO - 1 - k
        for row in range(-reach, ny + reach):
            v[k + 1, row % rows] = powered(k, row)
    total = [jnp.zeros((8, 128), F32) for _ in range(NMOM * len(SHIFTS))]
    for y in range(ny):
        scaling = scaling_own[y]
        last = powered(ITERS - 1, y)
        for a in range(0, nx, 8):
            for b in range(0, nz, 128):
                m = scaling[a : a + 8, b : b + 128]
                base = [v[k, y, a : a + 8, b : b + 128] for k in range(ITERS)] + [last[a : a + 8, b : b + 128]]
                for i, mu in enumerate(SHIFTS):
                    level, shifted = base, [base[0]]
                    for _ in range(ITERS):
                        level = [hi - (lo if mu == 1.0 else mu * lo) for lo, hi in zip(level, level[1:])]
                        shifted.append(level[0])
                    for k in range(ITERS):
                        weighted = m * shifted[k]
                        n = i * NMOM + 2 * k
                        total[n] = total[n] + weighted * shifted[k]
                        total[n + 1] = total[n + 1] + weighted * shifted[k + 1]
    stacked = jnp.concatenate([jnp.sum(x, axis=0, keepdims=True) for x in total], axis=0)
    sums = jnp.sum(stacked, axis=1, keepdims=True)
    n = len(total)
    diagonal = iota((n, 128), 0) == iota((n, 128), 1)
    line = jnp.sum(jnp.where(diagonal, sums, 0.0), axis=0, keepdims=True)
    part[...] = jnp.broadcast_to(line[None], part.shape)


def coefficients(moments):
    nearer = moments[1] + (SHIFTS[0] - SPLIT) * moments[0] < 0.0
    mom = [jnp.where(nearer, a, b) for a, b in zip(moments[:NMOM], moments[NMOM:])]
    mu = jnp.where(nearer, SHIFTS[0], SHIFTS[1]).astype(F32)
    zero = jnp.zeros_like(mom[0])
    one = zero + 1.0

    def times(poly):
        return [(lo + mu * hi) for lo, hi in zip([zero] + poly, poly + [zero])]

    sigma, tau = mom, mom
    rho, pi, x = [one], [one], [zero] * ITERS
    energy, lead = mom[0], one
    for k in range(ITERS):
        image = [hi + mu * lo for lo, hi in zip(tau, tau[1:])]
        step = energy / (lead * image[k])
        step = jnp.where((step > 0.4) & (step < 200.0), step, 0.0)
        x = [a + step * b for a, b in zip(x, pi + [zero] * (ITERS - len(pi)))]
        if k + 1 < ITERS:
            sigma = [a - step * b for a, b in zip(sigma, image)]
            rho = [a - step * b for a, b in zip(rho + [zero], times(pi))]
            lead = lead * -step
            fresh = lead * sigma[k + 1]
            fresh = jnp.maximum(fresh, 0.0)
            grow = jnp.where(energy > 0.0, fresh / energy, 0.0)
            tau = [a + grow * b for a, b in zip(sigma, tau)]
            pi = [a + grow * b for a, b in zip(rho, pi + [zero])]
            energy = fresh
    for i in range(ITERS - 1):
        for j in range(ITERS - 2, i - 1, -1):
            x[j] = x[j] - mu * x[j + 1]
    return x


def finish_kernel(parts, v, cot, vel, adj):
    _, ny, nx, nz = cot.shape
    line = jnp.sum(parts[...], axis=0)
    spread = jnp.broadcast_to(line, (8, 128))
    lane = iota((8, 128), 1)
    moments = [
        jnp.sum(jnp.where(lane == n, spread, 0.0), axis=1, keepdims=True) for n in range(NMOM * len(SHIFTS))
    ]
    coef = [c[:1] for c in coefficients(moments)]
    lane = iota((nx, nz), 1)

    def pressure(row):
        total = coef[0] * v[0, row]
        for k in range(1, ITERS):
            total = total + coef[k] * v[k, row]
        return total

    here = pressure(0)
    for y in range(ny):
        above = pressure(y + 1)
        x = here[:nx]
        adj[y] = x
        vel[0, y] = cot[0, y] + above[:nx] - x
        vel[1, y] = cot[1, y] + pltpu.roll(here, nx + 7, 0)[:nx] - x
        vel[2, y] = cot[2, y] + jnp.where(lane == nz - 1, 0.0, pltpu.roll(x, nz - 1, 1)) - x
        here = above


def neighbour(x, dy, dx, ny, nx):
    pairs = [
        (a * nx + b, (a + dy) * nx + b + dx)
        for a in range(ny)
        for b in range(nx)
        if 0 <= a + dy < ny and 0 <= b + dx < nx
    ]
    return lax.ppermute(x, AXES, pairs)


def exchange_sum(x, axes):
    return jnp.sum(lax.all_to_all(x, axes, 0, 0), axis=0, keepdims=True)


def on_device(gy, gx, sizes, cotangent, coefficient):
    ny, nx, nz = coefficient.shape
    limit = pltpu.CompilerParams(vmem_limit_bytes=24 * 1024 * 1024)
    send = functools.partial(neighbour, ny=gy, nx=gx)

    def shapes(*sizes):
        return [jax.ShapeDtypeStruct(s, F32) for s in sizes]

    rows, wide = ny + 2 * HALO, nx + 8
    block = (ny, nx, nz)
    t, d, scaling, up, down = pl.pallas_call(
        pack_kernel,
        in_specs=[pl.BlockSpec(memory_space=pltpu.HBM)] * 2,
        out_shape=shapes(block, block, block, (2 * HALO + 2, nx, nz), (2 * HALO + 1, nx, nz)),
        scratch_shapes=[
            pltpu.VMEM(cotangent.shape, F32),
            pltpu.VMEM(block, F32),
            pltpu.SemaphoreType.DMA((2,)),
        ],
        compiler_params=limit,
        name="pack",
    )(cotangent, coefficient)
    r_s = send(up, 1, 0)
    r_n = send(down, -1, 0)
    right, left = pl.pallas_call(
        side_kernel,
        out_shape=shapes((rows + 2, 8, nz), (rows, 8, nz)),
        compiler_params=limit,
        name="side",
    )(t, d, up, r_s, r_n)
    r_l = send(right, 0, 1)
    r_r = send(left, 0, -1)
    first, second = (int(np.prod([sizes[a] for a in axes])) for axes in STAGE)
    v, part = pl.pallas_call(
        krylov_kernel,
        out_shape=[
            jax.ShapeDtypeStruct((ITERS, rows, wide, nz), F32),
            jax.ShapeDtypeStruct((first, 1, 128), F32),
        ],
        scratch_shapes=[pltpu.VMEM((rows, wide, nz), F32)],
        compiler_params=limit,
        name="krylov",
    )(t, d, scaling, up, right, r_s, r_n, r_l, r_r)
    part = exchange_sum(part, STAGE[0])
    part = lax.all_to_all(jnp.broadcast_to(part, (second, 1, 128)), STAGE[1], 0, 0)
    return tuple(
        pl.pallas_call(
            finish_kernel,
            out_shape=[
                jax.ShapeDtypeStruct(cotangent.shape, F32),
                jax.ShapeDtypeStruct(coefficient.shape, F32),
            ],
            compiler_params=limit,
            name="finish",
        )(part, v, cotangent)
    )


def solution(mesh):
    gy, gx = mesh.shape["gy"], mesh.shape["gx"]
    fine = Mesh(np.asarray(mesh.devices).reshape(gy, gx // 32, 2, 8, 2), AXES)
    along_x = AXES[1:]
    wide, flat = P(None, AXES[0], along_x, None), P(AXES[0], along_x, None)
    return jax.shard_map(
        functools.partial(on_device, gy, gx, dict(fine.shape)),
        mesh=fine,
        in_specs=(wide, flat),
        out_specs=(wide, flat),
        check_vma=False,
    )
```

```python
import functools

import jax
import jax.numpy as jnp
import numpy as np
from jax import lax
from jax.experimental import pallas as pl
from jax.experimental.pallas import tpu as pltpu
from jax.sharding import Mesh, PartitionSpec as P

ITERS = 4
HALO = ITERS
SHIFTS = (0.25, 1.0)
SPLIT = 0.6
NMOM = 2 * ITERS
AXES = ("y", "xh", "xl", "z", "c")
STAGE = (("xh", "z"), ("y", "xl", "c"))
F32 = jnp.float32


def iota(shape, axis):
    return lax.broadcasted_iota(jnp.int32, shape, axis)


def pack_kernel(cot_hbm, coef_hbm, t_out, d_out, scaling, up, down, cot, coef, sems):
    copies = [
        pltpu.make_async_copy(coef_hbm, coef, sems.at[0]),
        pltpu.make_async_copy(cot_hbm, cot, sems.at[1]),
    ]
    for copy in copies:
        copy.start()
    for copy in copies:
        copy.wait()
    ny, nx, nz = coef.shape
    sub, lane = iota((nx, nz), 0), iota((nx, nz), 1)
    column = jnp.zeros((nx, nz), F32)
    for y in range(ny):
        c0, c1, c2 = cot[0, y], cot[1, y], cot[2, y]
        m = 6.0 + coef[y]
        d = 1.0 / m
        t = jnp.where(sub == 0, 0.0, pltpu.roll(c1, 1, 0)) - c1
        t = t + (jnp.where(lane == 0, 0.0, pltpu.roll(c2, 1, 1)) - c2)
        t = t + ((cot[0, y - 1] - c0) if y else -c0)
        t_out[y] = t
        d_out[y] = d
        scaling[y] = m
        if y < HALO:
            down[y], down[HALO + y] = t, d
        if y >= ny - HALO:
            j = y - (ny - HALO)
            up[j], up[HALO + j] = t, d
        column = jnp.where(sub == y, jnp.broadcast_to(c1[nx - 1 : nx], (nx, nz)), column)
    up[2 * HALO] = cot[0, ny - 1]
    up[2 * HALO + 1] = column
    down[2 * HALO] = column


def window_rows(t_own, d_own, up, r_s, r_n):
    ny = t_own.shape[0]
    out = []
    for y in range(ny):
        t = t_own[y]
        out.append((t + r_s[2 * HALO] if y == 0 else t, d_own[y]))
    for j in range(HALO):
        t = r_n[j]
        out.append((t + up[2 * HALO] if j == 0 else t, r_n[HALO + j]))
    return out + [(r_s[j], r_s[HALO + j]) for j in range(HALO)]


def side_kernel(odd, t_own, d_own, up, r_s, r_n, to_core, to_chip):
    ny, nx, nz = t_own.shape
    low = iota((8, nz), 0) < 4
    even = odd[0] == 0
    for row, (t, d) in enumerate(window_rows(t_own, d_own, up, r_s, r_n)):
        right = jnp.where(low, pltpu.roll(d[nx - 8 :], 4, 0), t[nx - 8 :])
        left = jnp.where(low, t[:8], pltpu.roll(d[:8], 4, 0))
        to_core[row] = jnp.where(even, right, left)
        to_chip[row] = jnp.where(even, left, right)
    rows = ny + 2 * HALO
    for to in (to_core, to_chip):
        to[rows] = up[2 * HALO + 1, :8]
        to[rows + 1] = jnp.where(low, r_n[2 * HALO, :8], r_s[2 * HALO + 1, :8])


def krylov_kernel(odd, t_own, d_own, scaling_own, up, to_core, r_s, r_n, r_core, r_chip, v, part, dw):
    ny, nx, nz = t_own.shape
    sub8 = iota((8, nz), 0)
    lane = iota((nx + 8, nz), 1)
    low = sub8 < 4
    even = odd[0] == 0

    def from_left(row):
        return jnp.where(even, r_chip[row], r_core[row])

    def from_right(row):
        return jnp.where(even, r_core[row], r_chip[row])

    columns = [(from_left(ny + 2 * HALO + i), to_core[ny + 2 * HALO + i]) for i in range(2)]

    def at_first(column, k):
        return jnp.where(sub8 == 0, jnp.broadcast_to(column[k : k + 1], (8, nz)), 0.0)

    for row, (t, d) in enumerate(window_rows(t_own, d_own, up, r_s, r_n)):
        before, after = columns[row // 8]
        v[0, row, 0:8] = (t[:8] + at_first(before, row % 8)) * d[:8]
        v[0, row, 8:nx] = t[8:] * d[8:]
        left, right = from_left(row), from_right(row)
        t = jnp.where(low, right, left) + at_first(after, row % 8)
        d_side = pltpu.roll(jnp.where(low, left, right), 4, 0)
        v[0, row, nx : nx + 8] = t * d_side
        dw[row, 0:nx] = d
        dw[row, nx : nx + 8] = d_side

    rows = ny + 2 * HALO

    def powered(k, row):
        row = row % rows
        x = v[k, row]
        beside = v[k, (row + 1) % rows] + v[k, (row - 1) % rows]
        beside = beside + (pltpu.roll(x, 1, 0) + pltpu.roll(x, nx + 7, 0))
        beside = beside + jnp.where(lane == 0, 0.0, pltpu.roll(x, 1, 1))
        beside = beside + jnp.where(lane == nz - 1, 0.0, pltpu.roll(x, nz - 1, 1))
        return x - dw[row] * beside

    for k in range(ITERS - 1):
        reach = HALO - 1 - k
        for row in range(-reach, ny + reach):
            v[k + 1, row % rows] = powered(k, row)
    total = [jnp.zeros((8, 128), F32) for _ in range(NMOM * len(SHIFTS))]
    for y in range(ny):
        scaling = scaling_own[y]
        last = powered(ITERS - 1, y)
        for a in range(0, nx, 8):
            for b in range(0, nz, 128):
                m = scaling[a : a + 8, b : b + 128]
                base = [v[k, y, a : a + 8, b : b + 128] for k in range(ITERS)] + [last[a : a + 8, b : b + 128]]
                for i, mu in enumerate(SHIFTS):
                    level, shifted = base, [base[0]]
                    for _ in range(ITERS):
                        level = [hi - (lo if mu == 1.0 else mu * lo) for lo, hi in zip(level, level[1:])]
                        shifted.append(level[0])
                    for k in range(ITERS):
                        weighted = m * shifted[k]
                        n = i * NMOM + 2 * k
                        total[n] = total[n] + weighted * shifted[k]
                        total[n + 1] = total[n + 1] + weighted * shifted[k + 1]
    stacked = jnp.concatenate([jnp.sum(x, axis=0, keepdims=True) for x in total], axis=0)
    sums = jnp.sum(stacked, axis=1, keepdims=True)
    n = len(total)
    diagonal = iota((n, 128), 0) == iota((n, 128), 1)
    line = jnp.sum(jnp.where(diagonal, sums, 0.0), axis=0, keepdims=True)
    part[...] = jnp.broadcast_to(line[None], part.shape)


def coefficients(moments):
    nearer = moments[1] + (SHIFTS[0] - SPLIT) * moments[0] < 0.0
    mom = [jnp.where(nearer, a, b) for a, b in zip(moments[:NMOM], moments[NMOM:])]
    mu = jnp.where(nearer, SHIFTS[0], SHIFTS[1]).astype(F32)
    zero = jnp.zeros_like(mom[0])
    one = zero + 1.0

    def times(poly):
        return [(lo + mu * hi) for lo, hi in zip([zero] + poly, poly + [zero])]

    sigma, tau = mom, mom
    rho, pi, x = [one], [one], [zero] * ITERS
    energy, lead = mom[0], one
    for k in range(ITERS):
        image = [hi + mu * lo for lo, hi in zip(tau, tau[1:])]
        step = energy / (lead * image[k])
        step = jnp.where((step > 0.4) & (step < 200.0), step, 0.0)
        x = [a + step * b for a, b in zip(x, pi + [zero] * (ITERS - len(pi)))]
        if k + 1 < ITERS:
            sigma = [a - step * b for a, b in zip(sigma, image)]
            rho = [a - step * b for a, b in zip(rho + [zero], times(pi))]
            lead = lead * -step
            fresh = lead * sigma[k + 1]
            fresh = jnp.maximum(fresh, 0.0)
            grow = jnp.where(energy > 0.0, fresh / energy, 0.0)
            tau = [a + grow * b for a, b in zip(sigma, tau)]
            pi = [a + grow * b for a, b in zip(rho, pi + [zero])]
            energy = fresh
    for i in range(ITERS - 1):
        for j in range(ITERS - 2, i - 1, -1):
            x[j] = x[j] - mu * x[j + 1]
    return x


def finish_kernel(parts, v, cot, vel, adj):
    _, ny, nx, nz = cot.shape
    line = jnp.sum(parts[...], axis=0)
    spread = jnp.broadcast_to(line, (8, 128))
    lane = iota((8, 128), 1)
    moments = [
        jnp.sum(jnp.where(lane == n, spread, 0.0), axis=1, keepdims=True) for n in range(NMOM * len(SHIFTS))
    ]
    coef = [c[:1] for c in coefficients(moments)]
    lane = iota((nx, nz), 1)

    def pressure(row):
        total = coef[0] * v[0, row]
        for k in range(1, ITERS):
            total = total + coef[k] * v[k, row]
        return total

    here = pressure(0)
    for y in range(ny):
        above = pressure(y + 1)
        x = here[:nx]
        adj[y] = x
        vel[0, y] = cot[0, y] + above[:nx] - x
        vel[1, y] = cot[1, y] + pltpu.roll(here, nx + 7, 0)[:nx] - x
        vel[2, y] = cot[2, y] + jnp.where(lane == nz - 1, 0.0, pltpu.roll(x, nz - 1, 1)) - x
        here = above


def along_y(x, dy, ny, nx):
    return lax.ppermute(x, AXES, [(a * nx + b, (a + dy) * nx + b) for a in range(ny) for b in range(nx) if 0 <= a + dy < ny])


def pairs_along_x(x, first, ny, nx):
    up = [(a * nx + b, a * nx + b + 1) for a in range(ny) for b in range(first, nx - 1, 2)]
    return lax.ppermute(x, AXES, up + [(j, i) for i, j in up])


def exchange_sum(x, axes):
    return jnp.sum(lax.all_to_all(x, axes, 0, 0), axis=0, keepdims=True)


def on_device(gy, gx, sizes, cotangent, coefficient):
    ny, nx, nz = coefficient.shape
    limit = pltpu.CompilerParams(vmem_limit_bytes=24 * 1024 * 1024)

    def shapes(*sizes):
        return [jax.ShapeDtypeStruct(s, F32) for s in sizes]

    rows, wide = ny + 2 * HALO, nx + 8
    block = (ny, nx, nz)
    t, d, scaling, up, down = pl.pallas_call(
        pack_kernel,
        in_specs=[pl.BlockSpec(memory_space=pltpu.HBM)] * 2,
        out_shape=shapes(block, block, block, (2 * HALO + 2, nx, nz), (2 * HALO + 1, nx, nz)),
        scratch_shapes=[
            pltpu.VMEM(cotangent.shape, F32),
            pltpu.VMEM(block, F32),
            pltpu.SemaphoreType.DMA((2,)),
        ],
        compiler_params=limit,
        name="pack",
    )(cotangent, coefficient)
    r_s = along_y(up, 1, gy, gx)
    r_n = along_y(down, -1, gy, gx)
    odd = lax.axis_index("c").astype(jnp.int32).reshape(1)
    scalar = pl.BlockSpec(memory_space=pltpu.SMEM)
    whole = pl.BlockSpec(memory_space=pltpu.VMEM)
    side = (rows + 2, 8, nz)
    to_core, to_chip = pl.pallas_call(
        side_kernel,
        in_specs=[scalar] + [whole] * 5,
        out_shape=shapes(side, side),
        compiler_params=limit,
        name="side",
    )(odd, t, d, up, r_s, r_n)
    r_chip = pairs_along_x(to_chip, 1, gy, gx)
    r_core = pairs_along_x(to_core, 0, gy, gx)
    first, second = (int(np.prod([sizes[a] for a in axes])) for axes in STAGE)
    v, part = pl.pallas_call(
        krylov_kernel,
        in_specs=[scalar] + [whole] * 9,
        out_shape=[
            jax.ShapeDtypeStruct((ITERS, rows, wide, nz), F32),
            jax.ShapeDtypeStruct((first, 1, 128), F32),
        ],
        scratch_shapes=[pltpu.VMEM((rows, wide, nz), F32)],
        compiler_params=limit,
        name="krylov",
    )(odd, t, d, scaling, up, to_core, r_s, r_n, r_core, r_chip)
    part = exchange_sum(part, STAGE[0])
    part = lax.all_to_all(jnp.broadcast_to(part, (second, 1, 128)), STAGE[1], 0, 0)
    return tuple(
        pl.pallas_call(
            finish_kernel,
            out_shape=[
                jax.ShapeDtypeStruct(cotangent.shape, F32),
                jax.ShapeDtypeStruct(coefficient.shape, F32),
            ],
            compiler_params=limit,
            name="finish",
        )(part, v, cotangent)
    )


def solution(mesh):
    gy, gx = mesh.shape["gy"], mesh.shape["gx"]
    fine = Mesh(np.asarray(mesh.devices).reshape(gy, gx // 32, 2, 8, 2), AXES)
    along_x = AXES[1:]
    wide, flat = P(None, AXES[0], along_x, None), P(AXES[0], along_x, None)
    return jax.shard_map(
        functools.partial(on_device, gy, gx, dict(fine.shape)),
        mesh=fine,
        in_specs=(wide, flat),
        out_specs=(wide, flat),
        check_vma=False,
    )
```

```python
import functools

import jax
import jax.numpy as jnp
import numpy as np
from jax import lax
from jax.experimental import pallas as pl
from jax.experimental.pallas import tpu as pltpu
from jax.sharding import Mesh, PartitionSpec as P

ITERS = 4
HALO = ITERS
SHIFTS = (0.25, 1.0)
SPLIT = 0.6
NMOM = 2 * ITERS
AXES = ("y", "xh", "xl", "z", "c")
STAGE = (("y", "xl", "c"), ("xh", "z"))
F32 = jnp.float32


def iota(shape, axis):
    return lax.broadcasted_iota(jnp.int32, shape, axis)


def pack_kernel(cot, scaling, t_out, d_out, up, down):
    ny, nx, nz = scaling.shape
    sub, lane = iota((nx, nz), 0), iota((nx, nz), 1)
    column = jnp.zeros((nx, nz), F32)
    for y in range(ny):
        c0, c1, c2 = cot[0, y], cot[1, y], cot[2, y]
        d = 1.0 / scaling[y]
        t = jnp.where(sub == 0, 0.0, pltpu.roll(c1, 1, 0)) - c1
        t = t + (jnp.where(lane == 0, 0.0, pltpu.roll(c2, 1, 1)) - c2)
        t = t + ((cot[0, y - 1] - c0) if y else -c0)
        t_out[y] = t
        d_out[y] = d
        if y < HALO:
            down[y], down[HALO + y] = t, d
        if y >= ny - HALO:
            j = y - (ny - HALO)
            up[j], up[HALO + j] = t, d
        column = jnp.where(sub == y, jnp.broadcast_to(c1[nx - 1 : nx], (nx, nz)), column)
    up[2 * HALO] = cot[0, ny - 1]
    up[2 * HALO + 1] = column
    down[2 * HALO] = column


def window_rows(t_own, d_own, up, r_s, r_n):
    ny = t_own.shape[0]
    out = []
    for y in range(ny):
        t = t_own[y]
        out.append((t + r_s[2 * HALO] if y == 0 else t, d_own[y]))
    for j in range(HALO):
        t = r_n[j]
        out.append((t + up[2 * HALO] if j == 0 else t, r_n[HALO + j]))
    return out + [(r_s[j], r_s[HALO + j]) for j in range(HALO)]


def side_kernel(odd, t_own, d_own, up, r_s, r_n, to_core, to_chip):
    ny, nx, nz = t_own.shape
    low = iota((8, nz), 0) < 4
    even = odd[0] == 0
    for row, (t, d) in enumerate(window_rows(t_own, d_own, up, r_s, r_n)):
        right = jnp.where(low, pltpu.roll(d[nx - 8 :], 4, 0), t[nx - 8 :])
        left = jnp.where(low, t[:8], pltpu.roll(d[:8], 4, 0))
        to_core[row] = jnp.where(even, right, left)
        to_chip[row] = jnp.where(even, left, right)
    rows = ny + 2 * HALO
    for to in (to_core, to_chip):
        to[rows] = up[2 * HALO + 1, :8]
        to[rows + 1] = jnp.where(low, r_n[2 * HALO, :8], r_s[2 * HALO + 1, :8])


def krylov_kernel(odd, t_own, d_own, scaling_own, up, to_core, r_s, r_n, r_core, r_chip, v, part, dw):
    ny, nx, nz = t_own.shape
    sub8 = iota((8, nz), 0)
    lane = iota((nx + 8, nz), 1)
    low = sub8 < 4
    even = odd[0] == 0

    def from_left(row):
        return jnp.where(even, r_chip[row], r_core[row])

    def from_right(row):
        return jnp.where(even, r_core[row], r_chip[row])

    columns = [(from_left(ny + 2 * HALO + i), to_core[ny + 2 * HALO + i]) for i in range(2)]

    def at_first(column, k):
        return jnp.where(sub8 == 0, jnp.broadcast_to(column[k : k + 1], (8, nz)), 0.0)

    for row, (t, d) in enumerate(window_rows(t_own, d_own, up, r_s, r_n)):
        before, after = columns[row // 8]
        v[0, row, 0:8] = (t[:8] + at_first(before, row % 8)) * d[:8]
        v[0, row, 8:nx] = t[8:] * d[8:]
        left, right = from_left(row), from_right(row)
        t = jnp.where(low, right, left) + at_first(after, row % 8)
        d_side = pltpu.roll(jnp.where(low, left, right), 4, 0)
        v[0, row, nx : nx + 8] = t * d_side
        dw[row, 0:nx] = d
        dw[row, nx : nx + 8] = d_side

    rows = ny + 2 * HALO

    def powered(k, row):
        row = row % rows
        x = v[k, row]
        beside = v[k, (row + 1) % rows] + v[k, (row - 1) % rows]
        beside = beside + (pltpu.roll(x, 1, 0) + pltpu.roll(x, nx + 7, 0))
        beside = beside + jnp.where(lane == 0, 0.0, pltpu.roll(x, 1, 1))
        beside = beside + jnp.where(lane == nz - 1, 0.0, pltpu.roll(x, nz - 1, 1))
        return x - dw[row] * beside

    for k in range(ITERS - 1):
        reach = HALO - 1 - k
        for row in range(-reach, ny + reach):
            v[k + 1, row % rows] = powered(k, row)
    total = [jnp.zeros((8, 128), F32) for _ in range(NMOM * len(SHIFTS))]
    for y in range(ny):
        scaling = scaling_own[y]
        last = powered(ITERS - 1, y)
        for a in range(0, nx, 8):
            for b in range(0, nz, 128):
                m = scaling[a : a + 8, b : b + 128]
                base = [v[k, y, a : a + 8, b : b + 128] for k in range(ITERS)] + [last[a : a + 8, b : b + 128]]
                for i, mu in enumerate(SHIFTS):
                    level, shifted = base, [base[0]]
                    for _ in range(ITERS):
                        level = [hi - (lo if mu == 1.0 else mu * lo) for lo, hi in zip(level, level[1:])]
                        shifted.append(level[0])
                    for k in range(ITERS):
                        weighted = m * shifted[k]
                        n = i * NMOM + 2 * k
                        total[n] = total[n] + weighted * shifted[k]
                        total[n + 1] = total[n + 1] + weighted * shifted[k + 1]
    stacked = jnp.concatenate([jnp.sum(x, axis=0, keepdims=True) for x in total], axis=0)
    sums = jnp.sum(stacked, axis=1, keepdims=True)
    n = len(total)
    diagonal = iota((n, 128), 0) == iota((n, 128), 1)
    line = jnp.sum(jnp.where(diagonal, sums, 0.0), axis=0, keepdims=True)
    part[...] = jnp.broadcast_to(line[None], part.shape)


def coefficients(moments):
    nearer = moments[1] + (SHIFTS[0] - SPLIT) * moments[0] < 0.0
    mom = [jnp.where(nearer, a, b) for a, b in zip(moments[:NMOM], moments[NMOM:])]
    mu = jnp.where(nearer, SHIFTS[0], SHIFTS[1]).astype(F32)
    zero = jnp.zeros_like(mom[0])
    one = zero + 1.0

    def times(poly):
        return [(lo + mu * hi) for lo, hi in zip([zero] + poly, poly + [zero])]

    sigma, tau = mom, mom
    rho, pi, x = [one], [one], [zero] * ITERS
    energy, lead = mom[0], one
    for k in range(ITERS):
        image = [hi + mu * lo for lo, hi in zip(tau, tau[1:])]
        step = energy / (lead * image[k])
        step = jnp.where((step > 0.4) & (step < 200.0), step, 0.0)
        x = [a + step * b for a, b in zip(x, pi + [zero] * (ITERS - len(pi)))]
        if k + 1 < ITERS:
            sigma = [a - step * b for a, b in zip(sigma, image)]
            rho = [a - step * b for a, b in zip(rho + [zero], times(pi))]
            lead = lead * -step
            fresh = lead * sigma[k + 1]
            fresh = jnp.maximum(fresh, 0.0)
            grow = jnp.where(energy > 0.0, fresh / energy, 0.0)
            tau = [a + grow * b for a, b in zip(sigma, tau)]
            pi = [a + grow * b for a, b in zip(rho, pi + [zero])]
            energy = fresh
    for i in range(ITERS - 1):
        for j in range(ITERS - 2, i - 1, -1):
            x[j] = x[j] - mu * x[j + 1]
    return x


def finish_kernel(parts, v, cot, vel, adj):
    _, ny, nx, nz = cot.shape
    line = jnp.sum(parts[...], axis=0)
    spread = jnp.broadcast_to(line, (8, 128))
    lane = iota((8, 128), 1)
    moments = [
        jnp.sum(jnp.where(lane == n, spread, 0.0), axis=1, keepdims=True) for n in range(NMOM * len(SHIFTS))
    ]
    coef = [c[:1] for c in coefficients(moments)]
    lane = iota((nx, nz), 1)

    def pressure(row):
        total = coef[0] * v[0, row]
        for k in range(1, ITERS):
            total = total + coef[k] * v[k, row]
        return total

    here = pressure(0)
    for y in range(ny):
        above = pressure(y + 1)
        x = here[:nx]
        adj[y] = x
        vel[0, y] = cot[0, y] + above[:nx] - x
        vel[1, y] = cot[1, y] + pltpu.roll(here, nx + 7, 0)[:nx] - x
        vel[2, y] = cot[2, y] + jnp.where(lane == nz - 1, 0.0, pltpu.roll(x, nz - 1, 1)) - x
        here = above


def along_y(x, dy, ny, nx):
    return lax.ppermute(x, AXES, [(a * nx + b, (a + dy) * nx + b) for a in range(ny) for b in range(nx) if 0 <= a + dy < ny])


def pairs_along_x(x, first, ny, nx):
    up = [(a * nx + b, a * nx + b + 1) for a in range(ny) for b in range(first, nx - 1, 2)]
    return lax.ppermute(x, AXES, up + [(j, i) for i, j in up])


def exchange_sum(x, axes):
    return jnp.sum(lax.all_to_all(x, axes, 0, 0), axis=0, keepdims=True)


def on_device(gy, gx, sizes, cotangent, coefficient):
    ny, nx, nz = coefficient.shape
    limit = pltpu.CompilerParams(vmem_limit_bytes=24 * 1024 * 1024)

    def shapes(*sizes):
        return [jax.ShapeDtypeStruct(s, F32) for s in sizes]

    rows, wide = ny + 2 * HALO, nx + 8
    block = (ny, nx, nz)
    scaling = 6.0 + coefficient
    t, d, up, down = pl.pallas_call(
        pack_kernel,
        out_shape=shapes(block, block, (2 * HALO + 2, nx, nz), (2 * HALO + 1, nx, nz)),
        compiler_params=limit,
        name="pack",
    )(cotangent, scaling)
    r_s = along_y(up, 1, gy, gx)
    r_n = along_y(down, -1, gy, gx)
    odd = lax.axis_index("c").astype(jnp.int32).reshape(1)
    scalar = pl.BlockSpec(memory_space=pltpu.SMEM)
    whole = pl.BlockSpec(memory_space=pltpu.VMEM)
    side = (rows + 2, 8, nz)
    to_core, to_chip = pl.pallas_call(
        side_kernel,
        in_specs=[scalar] + [whole] * 5,
        out_shape=shapes(side, side),
        compiler_params=limit,
        name="side",
    )(odd, t, d, up, r_s, r_n)
    r_chip = pairs_along_x(to_chip, 1, gy, gx)
    r_core = pairs_along_x(to_core, 0, gy, gx)
    first, second = (int(np.prod([sizes[a] for a in axes])) for axes in STAGE)
    v, part = pl.pallas_call(
        krylov_kernel,
        in_specs=[scalar] + [whole] * 9,
        out_shape=[
            jax.ShapeDtypeStruct((ITERS, rows, wide, nz), F32),
            jax.ShapeDtypeStruct((first, 1, 128), F32),
        ],
        scratch_shapes=[pltpu.VMEM((rows, wide, nz), F32)],
        compiler_params=limit,
        name="krylov",
    )(odd, t, d, scaling, up, to_core, r_s, r_n, r_core, r_chip)
    part = exchange_sum(part, STAGE[0])
    part = lax.all_to_all(jnp.broadcast_to(part, (second, 1, 128)), STAGE[1], 0, 0)
    return tuple(
        pl.pallas_call(
            finish_kernel,
            out_shape=[
                jax.ShapeDtypeStruct(cotangent.shape, F32),
                jax.ShapeDtypeStruct(coefficient.shape, F32),
            ],
            compiler_params=limit,
            name="finish",
        )(part, v, cotangent)
    )


def solution(mesh):
    gy, gx = mesh.shape["gy"], mesh.shape["gx"]
    fine = Mesh(np.asarray(mesh.devices).reshape(gy, gx // 32, 2, 8, 2), AXES)
    along_x = AXES[1:]
    wide, flat = P(None, AXES[0], along_x, None), P(AXES[0], along_x, None)
    return jax.shard_map(
        functools.partial(on_device, gy, gx, dict(fine.shape)),
        mesh=fine,
        in_specs=(wide, flat),
        out_specs=(wide, flat),
        check_vma=False,
    )
```

```python
import functools

import jax
import jax.numpy as jnp
import numpy as np
from jax import lax
from jax.experimental import pallas as pl
from jax.experimental.pallas import tpu as pltpu
from jax.sharding import Mesh, PartitionSpec as P

ITERS = 4
HALO = ITERS
SHIFTS = (0.25, 1.0)
SPLIT = 0.6
NMOM = 2 * ITERS
AXES = ("y", "xh", "xl", "z", "c")
STAGE = (("y", "xl", "c"), ("xh", "z"))
F32 = jnp.float32


def iota(shape, axis):
    return lax.broadcasted_iota(jnp.int32, shape, axis)


def pack_kernel(fields, t_out, d_out, scaling, up, down):
    ny, nx, nz = t_out.shape
    sub, lane = iota((nx, nz), 0), iota((nx, nz), 1)
    column = jnp.zeros((nx, nz), F32)
    for y in range(ny):
        c0, c1, c2 = fields[0, y], fields[1, y], fields[2, y]
        m = 6.0 + fields[3, y]
        d = 1.0 / m
        scaling[y] = m
        t = jnp.where(sub == 0, 0.0, pltpu.roll(c1, 1, 0)) - c1
        t = t + (jnp.where(lane == 0, 0.0, pltpu.roll(c2, 1, 1)) - c2)
        t = t + ((fields[0, y - 1] - c0) if y else -c0)
        t_out[y] = t
        d_out[y] = d
        if y < HALO:
            down[y], down[HALO + y] = t, d
        if y >= ny - HALO:
            j = y - (ny - HALO)
            up[j], up[HALO + j] = t, d
        column = jnp.where(sub == y, jnp.broadcast_to(c1[nx - 1 : nx], (nx, nz)), column)
    up[2 * HALO] = fields[0, ny - 1]
    up[2 * HALO + 1] = column
    down[2 * HALO] = column


def window_rows(t_own, d_own, up, r_s, r_n):
    ny = t_own.shape[0]
    out = []
    for y in range(ny):
        t = t_own[y]
        out.append((t + r_s[2 * HALO] if y == 0 else t, d_own[y]))
    for j in range(HALO):
        t = r_n[j]
        out.append((t + up[2 * HALO] if j == 0 else t, r_n[HALO + j]))
    return out + [(r_s[j], r_s[HALO + j]) for j in range(HALO)]


def side_kernel(odd, t_own, d_own, up, r_s, r_n, to_core, to_chip):
    ny, nx, nz = t_own.shape
    low = iota((8, nz), 0) < 4
    even = odd[0] == 0
    for row, (t, d) in enumerate(window_rows(t_own, d_own, up, r_s, r_n)):
        right = jnp.where(low, pltpu.roll(d[nx - 8 :], 4, 0), t[nx - 8 :])
        left = jnp.where(low, t[:8], pltpu.roll(d[:8], 4, 0))
        to_core[row] = jnp.where(even, right, left)
        to_chip[row] = jnp.where(even, left, right)
    rows = ny + 2 * HALO
    for to in (to_core, to_chip):
        to[rows] = up[2 * HALO + 1, :8]
        to[rows + 1] = jnp.where(low, r_n[2 * HALO, :8], r_s[2 * HALO + 1, :8])


def krylov_kernel(odd, t_own, d_own, scaling_own, up, to_core, r_s, r_n, r_core, r_chip, v, part, dw):
    ny, nx, nz = t_own.shape
    sub8 = iota((8, nz), 0)
    lane = iota((nx + 8, nz), 1)
    low = sub8 < 4
    even = odd[0] == 0

    def from_left(row):
        return jnp.where(even, r_chip[row], r_core[row])

    def from_right(row):
        return jnp.where(even, r_core[row], r_chip[row])

    columns = [(from_left(ny + 2 * HALO + i), to_core[ny + 2 * HALO + i]) for i in range(2)]

    def at_first(column, k):
        return jnp.where(sub8 == 0, jnp.broadcast_to(column[k : k + 1], (8, nz)), 0.0)

    for row, (t, d) in enumerate(window_rows(t_own, d_own, up, r_s, r_n)):
        before, after = columns[row // 8]
        v[0, row, 0:8] = (t[:8] + at_first(before, row % 8)) * d[:8]
        v[0, row, 8:nx] = t[8:] * d[8:]
        left, right = from_left(row), from_right(row)
        t = jnp.where(low, right, left) + at_first(after, row % 8)
        d_side = pltpu.roll(jnp.where(low, left, right), 4, 0)
        v[0, row, nx : nx + 8] = t * d_side
        dw[row, 0:nx] = d
        dw[row, nx : nx + 8] = d_side

    rows = ny + 2 * HALO

    def powered(k, row):
        row = row % rows
        x = v[k, row]
        beside = v[k, (row + 1) % rows] + v[k, (row - 1) % rows]
        beside = beside + (pltpu.roll(x, 1, 0) + pltpu.roll(x, nx + 7, 0))
        beside = beside + jnp.where(lane == 0, 0.0, pltpu.roll(x, 1, 1))
        beside = beside + jnp.where(lane == nz - 1, 0.0, pltpu.roll(x, nz - 1, 1))
        return x - dw[row] * beside

    for k in range(ITERS - 1):
        reach = HALO - 1 - k
        for row in range(-reach, ny + reach):
            v[k + 1, row % rows] = powered(k, row)
    total = [jnp.zeros((8, 128), F32) for _ in range(NMOM * len(SHIFTS))]
    for y in range(ny):
        scaling = scaling_own[y]
        last = powered(ITERS - 1, y)
        for a in range(0, nx, 8):
            for b in range(0, nz, 128):
                m = scaling[a : a + 8, b : b + 128]
                base = [v[k, y, a : a + 8, b : b + 128] for k in range(ITERS)] + [last[a : a + 8, b : b + 128]]
                for i, mu in enumerate(SHIFTS):
                    level, shifted = base, [base[0]]
                    for _ in range(ITERS):
                        level = [hi - (lo if mu == 1.0 else mu * lo) for lo, hi in zip(level, level[1:])]
                        shifted.append(level[0])
                    for k in range(ITERS):
                        weighted = m * shifted[k]
                        n = i * NMOM + 2 * k
                        total[n] = total[n] + weighted * shifted[k]
                        total[n + 1] = total[n + 1] + weighted * shifted[k + 1]
    stacked = jnp.concatenate([jnp.sum(x, axis=0, keepdims=True) for x in total], axis=0)
    sums = jnp.sum(stacked, axis=1, keepdims=True)
    n = len(total)
    diagonal = iota((n, 128), 0) == iota((n, 128), 1)
    line = jnp.sum(jnp.where(diagonal, sums, 0.0), axis=0, keepdims=True)
    part[...] = jnp.broadcast_to(line[None], part.shape)


def coefficients(moments):
    nearer = moments[1] + (SHIFTS[0] - SPLIT) * moments[0] < 0.0
    mom = [jnp.where(nearer, a, b) for a, b in zip(moments[:NMOM], moments[NMOM:])]
    mu = jnp.where(nearer, SHIFTS[0], SHIFTS[1]).astype(F32)
    zero = jnp.zeros_like(mom[0])
    one = zero + 1.0

    def times(poly):
        return [(lo + mu * hi) for lo, hi in zip([zero] + poly, poly + [zero])]

    sigma, tau = mom, mom
    rho, pi, x = [one], [one], [zero] * ITERS
    energy, lead = mom[0], one
    for k in range(ITERS):
        image = [hi + mu * lo for lo, hi in zip(tau, tau[1:])]
        step = energy / (lead * image[k])
        step = jnp.where((step > 0.4) & (step < 200.0), step, 0.0)
        x = [a + step * b for a, b in zip(x, pi + [zero] * (ITERS - len(pi)))]
        if k + 1 < ITERS:
            sigma = [a - step * b for a, b in zip(sigma, image)]
            rho = [a - step * b for a, b in zip(rho + [zero], times(pi))]
            lead = lead * -step
            fresh = lead * sigma[k + 1]
            fresh = jnp.maximum(fresh, 0.0)
            grow = jnp.where(energy > 0.0, fresh / energy, 0.0)
            tau = [a + grow * b for a, b in zip(sigma, tau)]
            pi = [a + grow * b for a, b in zip(rho, pi + [zero])]
            energy = fresh
    for i in range(ITERS - 1):
        for j in range(ITERS - 2, i - 1, -1):
            x[j] = x[j] - mu * x[j + 1]
    return x


def finish_kernel(parts, v, cot, vel, adj):
    ny, nx, nz = adj.shape
    line = jnp.sum(parts[...], axis=0)
    spread = jnp.broadcast_to(line, (8, 128))
    lane = iota((8, 128), 1)
    moments = [
        jnp.sum(jnp.where(lane == n, spread, 0.0), axis=1, keepdims=True) for n in range(NMOM * len(SHIFTS))
    ]
    coef = [c[:1] for c in coefficients(moments)]
    lane = iota((nx, nz), 1)

    def pressure(row):
        total = coef[0] * v[0, row]
        for k in range(1, ITERS):
            total = total + coef[k] * v[k, row]
        return total

    here = pressure(0)
    for y in range(ny):
        above = pressure(y + 1)
        x = here[:nx]
        adj[y] = x
        vel[0, y] = cot[0, y] + above[:nx] - x
        vel[1, y] = cot[1, y] + pltpu.roll(here, nx + 7, 0)[:nx] - x
        vel[2, y] = cot[2, y] + jnp.where(lane == nz - 1, 0.0, pltpu.roll(x, nz - 1, 1)) - x
        here = above


def along_y(x, dy, ny, nx):
    return lax.ppermute(x, AXES, [(a * nx + b, (a + dy) * nx + b) for a in range(ny) for b in range(nx) if 0 <= a + dy < ny])


def pairs_along_x(x, first, ny, nx):
    up = [(a * nx + b, a * nx + b + 1) for a in range(ny) for b in range(first, nx - 1, 2)]
    return lax.ppermute(x, AXES, up + [(j, i) for i, j in up])


def exchange_sum(x, axes):
    return jnp.sum(lax.all_to_all(x, axes, 0, 0), axis=0, keepdims=True)


def on_device(gy, gx, sizes, cotangent, coefficient):
    ny, nx, nz = coefficient.shape
    limit = pltpu.CompilerParams(vmem_limit_bytes=24 * 1024 * 1024)

    def shapes(*sizes):
        return [jax.ShapeDtypeStruct(s, F32) for s in sizes]

    rows, wide = ny + 2 * HALO, nx + 8
    block = (ny, nx, nz)
    fields = jnp.concatenate([cotangent, coefficient[None]], axis=0)
    t, d, scaling, up, down = pl.pallas_call(
        pack_kernel,
        out_shape=shapes(block, block, block, (2 * HALO + 2, nx, nz), (2 * HALO + 1, nx, nz)),
        compiler_params=limit,
        name="pack",
    )(fields)
    r_s = along_y(up, 1, gy, gx)
    r_n = along_y(down, -1, gy, gx)
    odd = lax.axis_index("c").astype(jnp.int32).reshape(1)
    scalar = pl.BlockSpec(memory_space=pltpu.SMEM)
    whole = pl.BlockSpec(memory_space=pltpu.VMEM)
    side = (rows + 2, 8, nz)
    to_core, to_chip = pl.pallas_call(
        side_kernel,
        in_specs=[scalar] + [whole] * 5,
        out_shape=shapes(side, side),
        compiler_params=limit,
        name="side",
    )(odd, t, d, up, r_s, r_n)
    r_chip = pairs_along_x(to_chip, 1, gy, gx)
    r_core = pairs_along_x(to_core, 0, gy, gx)
    first, second = (int(np.prod([sizes[a] for a in axes])) for axes in STAGE)
    v, part = pl.pallas_call(
        krylov_kernel,
        in_specs=[scalar] + [whole] * 9,
        out_shape=[
            jax.ShapeDtypeStruct((ITERS, rows, wide, nz), F32),
            jax.ShapeDtypeStruct((first, 1, 128), F32),
        ],
        scratch_shapes=[pltpu.VMEM((rows, wide, nz), F32)],
        compiler_params=limit,
        name="krylov",
    )(odd, t, d, scaling, up, to_core, r_s, r_n, r_core, r_chip)
    part = exchange_sum(part, STAGE[0])
    part = lax.all_to_all(jnp.broadcast_to(part, (second, 1, 128)), STAGE[1], 0, 0)
    return tuple(
        pl.pallas_call(
            finish_kernel,
            out_shape=[
                jax.ShapeDtypeStruct(cotangent.shape, F32),
                jax.ShapeDtypeStruct(coefficient.shape, F32),
            ],
            compiler_params=limit,
            name="finish",
        )(part, v, fields)
    )


def solution(mesh):
    gy, gx = mesh.shape["gy"], mesh.shape["gx"]
    fine = Mesh(np.asarray(mesh.devices).reshape(gy, gx // 32, 2, 8, 2), AXES)
    along_x = AXES[1:]
    wide, flat = P(None, AXES[0], along_x, None), P(AXES[0], along_x, None)
    return jax.shard_map(
        functools.partial(on_device, gy, gx, dict(fine.shape)),
        mesh=fine,
        in_specs=(wide, flat),
        out_specs=(wide, flat),
        check_vma=False,
    )
```

```python
import functools

import jax
import jax.numpy as jnp
import numpy as np
from jax import lax
from jax.experimental import pallas as pl
from jax.experimental.pallas import tpu as pltpu
from jax.sharding import Mesh, PartitionSpec as P

ITERS = 4
HALO = ITERS
SHIFTS = (0.25, 1.0)
SPLIT = 0.6
NMOM = 2 * ITERS
AXES = ("y", "xh", "xl", "z", "c")
STAGE = (("y", "xl", "c"), ("xh", "z"))
F32 = jnp.float32


def iota(shape, axis):
    return lax.broadcasted_iota(jnp.int32, shape, axis)


def pack_kernel(fields, t_out, d_out, scaling, up, down):
    ny, nx, nz = t_out.shape
    sub, lane = iota((nx, nz), 0), iota((nx, nz), 1)
    column = jnp.zeros((nx, nz), F32)
    for y in range(ny):
        c0, c1, c2 = fields[0, y], fields[1, y], fields[2, y]
        m = 6.0 + fields[3, y]
        d = 1.0 / m
        scaling[y] = m
        t = jnp.where(sub == 0, 0.0, pltpu.roll(c1, 1, 0)) - c1
        t = t + (jnp.where(lane == 0, 0.0, pltpu.roll(c2, 1, 1)) - c2)
        t = t + ((fields[0, y - 1] - c0) if y else -c0)
        t_out[y] = t
        d_out[y] = d
        if y < HALO:
            down[y], down[HALO + y] = t, d
        if y >= ny - HALO:
            j = y - (ny - HALO)
            up[j], up[HALO + j] = t, d
        column = jnp.where(sub == y, jnp.broadcast_to(c1[nx - 1 : nx], (nx, nz)), column)
    up[2 * HALO] = fields[0, ny - 1]
    up[2 * HALO + 1] = column
    down[2 * HALO] = column


def window_rows(t_own, d_own, up, r_s, r_n):
    ny = t_own.shape[0]
    out = []
    for y in range(ny):
        t = t_own[y]
        out.append((t + r_s[2 * HALO] if y == 0 else t, d_own[y]))
    for j in range(HALO):
        t = r_n[j]
        out.append((t + up[2 * HALO] if j == 0 else t, r_n[HALO + j]))
    return out + [(r_s[j], r_s[HALO + j]) for j in range(HALO)]


def sent_along_x(ny):
    return [row for row in range(ny + 2 * HALO) if row not in (ny + HALO - 1, ny + HALO)]


def side_kernel(odd, t_own, d_own, up, r_s, r_n, to_core, to_chip):
    ny, nx, nz = t_own.shape
    low = iota((8, nz), 0) < 4
    even = odd[0] == 0
    window = window_rows(t_own, d_own, up, r_s, r_n)
    for row, (t, d) in enumerate(window[k] for k in sent_along_x(ny)):
        right = jnp.where(low, pltpu.roll(d[nx - 8 :], 4, 0), t[nx - 8 :])
        left = jnp.where(low, t[:8], pltpu.roll(d[:8], 4, 0))
        to_core[row] = jnp.where(even, right, left)
        to_chip[row] = jnp.where(even, left, right)
    rows = ny + 2 * HALO - 2
    for to in (to_core, to_chip):
        to[rows] = up[2 * HALO + 1, :8]
        to[rows + 1] = jnp.where(low, r_n[2 * HALO, :8], r_s[2 * HALO + 1, :8])


def krylov_kernel(odd, t_own, d_own, scaling_own, up, to_core, r_s, r_n, r_core, r_chip, v, part, dw):
    ny, nx, nz = t_own.shape
    sub8 = iota((8, nz), 0)
    lane = iota((nx + 8, nz), 1)
    low = sub8 < 4
    even = odd[0] == 0

    def from_left(row):
        return jnp.where(even, r_chip[row], r_core[row])

    def from_right(row):
        return jnp.where(even, r_core[row], r_chip[row])

    sent = sent_along_x(ny)
    columns = [(from_left(len(sent) + i), to_core[len(sent) + i]) for i in range(2)]

    def at_first(column, k):
        return jnp.where(sub8 == 0, jnp.broadcast_to(column[k : k + 1], (8, nz)), 0.0)

    for row, (t, d) in enumerate(window_rows(t_own, d_own, up, r_s, r_n)):
        before, after = columns[row // 8]
        v[0, row, 0:8] = (t[:8] + at_first(before, row % 8)) * d[:8]
        v[0, row, 8:nx] = t[8:] * d[8:]
        dw[row, 0:nx] = d
        if row not in sent:
            v[0, row, nx : nx + 8] = jnp.zeros((8, nz), F32)
            dw[row, nx : nx + 8] = jnp.zeros((8, nz), F32)
            continue
        left, right = from_left(sent.index(row)), from_right(sent.index(row))
        t = jnp.where(low, right, left) + at_first(after, row % 8)
        d_side = pltpu.roll(jnp.where(low, left, right), 4, 0)
        v[0, row, nx : nx + 8] = t * d_side
        dw[row, nx : nx + 8] = d_side

    rows = ny + 2 * HALO

    def powered(k, row):
        row = row % rows
        x = v[k, row]
        beside = v[k, (row + 1) % rows] + v[k, (row - 1) % rows]
        beside = beside + (pltpu.roll(x, 1, 0) + pltpu.roll(x, nx + 7, 0))
        beside = beside + jnp.where(lane == 0, 0.0, pltpu.roll(x, 1, 1))
        beside = beside + jnp.where(lane == nz - 1, 0.0, pltpu.roll(x, nz - 1, 1))
        return x - dw[row] * beside

    for k in range(ITERS - 1):
        reach = HALO - 1 - k
        for row in range(-reach, ny + reach):
            v[k + 1, row % rows] = powered(k, row)
    total = [jnp.zeros((8, 128), F32) for _ in range(NMOM * len(SHIFTS))]
    for y in range(ny):
        scaling = scaling_own[y]
        last = powered(ITERS - 1, y)
        for a in range(0, nx, 8):
            for b in range(0, nz, 128):
                m = scaling[a : a + 8, b : b + 128]
                base = [v[k, y, a : a + 8, b : b + 128] for k in range(ITERS)] + [last[a : a + 8, b : b + 128]]
                for i, mu in enumerate(SHIFTS):
                    level, shifted = base, [base[0]]
                    for _ in range(ITERS):
                        level = [hi - (lo if mu == 1.0 else mu * lo) for lo, hi in zip(level, level[1:])]
                        shifted.append(level[0])
                    for k in range(ITERS):
                        weighted = m * shifted[k]
                        n = i * NMOM + 2 * k
                        total[n] = total[n] + weighted * shifted[k]
                        total[n + 1] = total[n + 1] + weighted * shifted[k + 1]
    stacked = jnp.concatenate([jnp.sum(x, axis=0, keepdims=True) for x in total], axis=0)
    sums = jnp.sum(stacked, axis=1, keepdims=True)
    n = len(total)
    diagonal = iota((n, 128), 0) == iota((n, 128), 1)
    line = jnp.sum(jnp.where(diagonal, sums, 0.0), axis=0, keepdims=True)
    part[...] = jnp.broadcast_to(line[None], part.shape)


def coefficients(moments):
    nearer = moments[1] + (SHIFTS[0] - SPLIT) * moments[0] < 0.0
    mom = [jnp.where(nearer, a, b) for a, b in zip(moments[:NMOM], moments[NMOM:])]
    mu = jnp.where(nearer, SHIFTS[0], SHIFTS[1]).astype(F32)
    zero = jnp.zeros_like(mom[0])
    one = zero + 1.0

    def times(poly):
        return [(lo + mu * hi) for lo, hi in zip([zero] + poly, poly + [zero])]

    sigma, tau = mom, mom
    rho, pi, x = [one], [one], [zero] * ITERS
    energy, lead = mom[0], one
    for k in range(ITERS):
        image = [hi + mu * lo for lo, hi in zip(tau, tau[1:])]
        step = energy / (lead * image[k])
        step = jnp.where((step > 0.4) & (step < 200.0), step, 0.0)
        x = [a + step * b for a, b in zip(x, pi + [zero] * (ITERS - len(pi)))]
        if k + 1 < ITERS:
            sigma = [a - step * b for a, b in zip(sigma, image)]
            rho = [a - step * b for a, b in zip(rho + [zero], times(pi))]
            lead = lead * -step
            fresh = lead * sigma[k + 1]
            fresh = jnp.maximum(fresh, 0.0)
            grow = jnp.where(energy > 0.0, fresh / energy, 0.0)
            tau = [a + grow * b for a, b in zip(sigma, tau)]
            pi = [a + grow * b for a, b in zip(rho, pi + [zero])]
            energy = fresh
    for i in range(ITERS - 1):
        for j in range(ITERS - 2, i - 1, -1):
            x[j] = x[j] - mu * x[j + 1]
    return x


def finish_kernel(parts, v, cot, vel, adj):
    ny, nx, nz = adj.shape
    line = jnp.sum(parts[...], axis=0)
    spread = jnp.broadcast_to(line, (8, 128))
    lane = iota((8, 128), 1)
    moments = [
        jnp.sum(jnp.where(lane == n, spread, 0.0), axis=1, keepdims=True) for n in range(NMOM * len(SHIFTS))
    ]
    coef = [c[:1] for c in coefficients(moments)]
    lane = iota((nx, nz), 1)

    def pressure(row):
        total = coef[0] * v[0, row]
        for k in range(1, ITERS):
            total = total + coef[k] * v[k, row]
        return total

    here = pressure(0)
    for y in range(ny):
        above = pressure(y + 1)
        x = here[:nx]
        adj[y] = x
        vel[0, y] = cot[0, y] + above[:nx] - x
        vel[1, y] = cot[1, y] + pltpu.roll(here, nx + 7, 0)[:nx] - x
        vel[2, y] = cot[2, y] + jnp.where(lane == nz - 1, 0.0, pltpu.roll(x, nz - 1, 1)) - x
        here = above


def along_y(x, dy, ny, nx):
    return lax.ppermute(x, AXES, [(a * nx + b, (a + dy) * nx + b) for a in range(ny) for b in range(nx) if 0 <= a + dy < ny])


def pairs_along_x(x, first, ny, nx):
    up = [(a * nx + b, a * nx + b + 1) for a in range(ny) for b in range(first, nx - 1, 2)]
    return lax.ppermute(x, AXES, up + [(j, i) for i, j in up])


def exchange_sum(x, axes):
    return jnp.sum(lax.all_to_all(x, axes, 0, 0), axis=0, keepdims=True)


def on_device(gy, gx, sizes, cotangent, coefficient):
    ny, nx, nz = coefficient.shape
    limit = pltpu.CompilerParams(vmem_limit_bytes=24 * 1024 * 1024)

    def shapes(*sizes):
        return [jax.ShapeDtypeStruct(s, F32) for s in sizes]

    rows, wide = ny + 2 * HALO, nx + 8
    block = (ny, nx, nz)
    fields = jnp.concatenate([cotangent, coefficient[None]], axis=0)
    t, d, scaling, up, down = pl.pallas_call(
        pack_kernel,
        out_shape=shapes(block, block, block, (2 * HALO + 2, nx, nz), (2 * HALO + 1, nx, nz)),
        compiler_params=limit,
        name="pack",
    )(fields)
    r_s = along_y(up, 1, gy, gx)
    r_n = along_y(down, -1, gy, gx)
    odd = lax.axis_index("c").astype(jnp.int32).reshape(1)
    scalar = pl.BlockSpec(memory_space=pltpu.SMEM)
    whole = pl.BlockSpec(memory_space=pltpu.VMEM)
    side = (rows, 8, nz)
    to_core, to_chip = pl.pallas_call(
        side_kernel,
        in_specs=[scalar] + [whole] * 5,
        out_shape=shapes(side, side),
        compiler_params=limit,
        name="side",
    )(odd, t, d, up, r_s, r_n)
    r_chip = pairs_along_x(to_chip, 1, gy, gx)
    r_core = pairs_along_x(to_core, 0, gy, gx)
    first, second = (int(np.prod([sizes[a] for a in axes])) for axes in STAGE)
    v, part = pl.pallas_call(
        krylov_kernel,
        in_specs=[scalar] + [whole] * 9,
        out_shape=[
            jax.ShapeDtypeStruct((ITERS, rows, wide, nz), F32),
            jax.ShapeDtypeStruct((first, 1, 128), F32),
        ],
        scratch_shapes=[pltpu.VMEM((rows, wide, nz), F32)],
        compiler_params=limit,
        name="krylov",
    )(odd, t, d, scaling, up, to_core, r_s, r_n, r_core, r_chip)
    part = exchange_sum(part, STAGE[0])
    part = lax.all_to_all(jnp.broadcast_to(part, (second, 1, 128)), STAGE[1], 0, 0)
    return tuple(
        pl.pallas_call(
            finish_kernel,
            out_shape=[
                jax.ShapeDtypeStruct(cotangent.shape, F32),
                jax.ShapeDtypeStruct(coefficient.shape, F32),
            ],
            compiler_params=limit,
            name="finish",
        )(part, v, fields)
    )


def solution(mesh):
    gy, gx = mesh.shape["gy"], mesh.shape["gx"]
    fine = Mesh(np.asarray(mesh.devices).reshape(gy, gx // 32, 2, 8, 2), AXES)
    along_x = AXES[1:]
    wide, flat = P(None, AXES[0], along_x, None), P(AXES[0], along_x, None)
    return jax.shard_map(
        functools.partial(on_device, gy, gx, dict(fine.shape)),
        mesh=fine,
        in_specs=(wide, flat),
        out_specs=(wide, flat),
        check_vma=False,
    )
```
